128 devices in a mesh: gx: 8 (over y, core), gy: 16 (over z, x).
Axes of the slice: x: 4, y: 4, z: 4, core: 2. Of those that a mesh axis runs over, the one named last changes fastest.
Arguments:
- level_set: float32 [512, 64, 4096], P(('gx', 'gy')), may hold values from -8 to 8
- tile_count: int32 [128], P(('gx', 'gy')), may hold values from 2 to 4, as said below
- neighbours: int32 [512, 6], P(('gx', 'gy')), may hold values from -1 to 7, as said below
Outputs:
- redistanced: float32 [512, 64, 4096], P(('gx', 'gy'))
The draws below stay inside these ranges and needn't reach their ends.
Inputs may be any that keep to these rules, and one draw needn't show every extreme that they name: Band tiles of a device fill its slots 0 to tile_count - 1; the other slots are empty. Some device holds 4. `neighbours`: -1 means no band tile on that face. A value n below 4 is slot n of the same device; a value n of 4 or more is slot n - 4 of the device one step lower along gx (face 0), higher along gx (face 1), lower along gy (face 2) or higher along gy (face 3), which exists; faces 4 and 5 (third dimension) are -1 or below 4. Every listed slot holds a band tile and is never the tile itself; empty slots list -1.
All inputs are finite; a program needn't handle non-finite values.
Results may differ from the reference program's by a relative error of at most 0.0003.
Values sent between devices are 32-bit elements; how exact they have to be, the bound alone decides.
A program may use at most 192 MiB of HBM per device.

```python
import jax
import jax.numpy as jnp
from jax import lax

EDGE = 64
SLOTS = 4
SHARE = 1
ALL_TILES = 512
N_GX = 8
N_GY = 16


def plan_counts(key):
    lowest = max(2, SLOTS // 4)
    counts = jax.random.randint(jax.random.fold_in(key, 101), (N_GX, N_GY), lowest, SLOTS - SHARE + 1)
    half_span = N_GY // 2
    chosen_row = jax.random.randint(jax.random.fold_in(key, 102), (), 0, N_GX)
    chosen_col = jax.random.randint(jax.random.fold_in(key, 103), (), 0, half_span)
    row_grid = jnp.arange(N_GX)[:, None]
    col_grid = jnp.arange(N_GY)[None, :]
    busiest = (row_grid == chosen_row) & (col_grid == chosen_col)
    lighter = (row_grid == chosen_row) & (col_grid == chosen_col + half_span)
    counts = jnp.where(busiest, SLOTS, counts)
    counts = jnp.where(lighter, SLOTS - 2 * SHARE, counts)
    return counts.reshape(N_GX * N_GY).astype(jnp.int32)


def draw_tile_count(key, part):
    return plan_counts(key)


def draw_neighbours(key, part):
    counts = plan_counts(key)
    key = jax.random.fold_in(key, 7)
    tile_total = N_GX * N_GY * SLOTS
    tile_ids = jnp.arange(tile_total)
    device = tile_ids // SLOTS
    slot_index = tile_ids % SLOTS
    grid_x = device // N_GY
    grid_y = device % N_GY
    own_count = counts[device]
    face_kinds = jax.random.randint(jax.random.fold_in(key, 1), (tile_total, 6), 0, 3)
    pick_local = jax.random.randint(jax.random.fold_in(key, 2), (tile_total, 6), 0, 1 << 20)
    pick_remote = jax.random.randint(jax.random.fold_in(key, 3), (tile_total, 6), 0, 1 << 20)
    offsets = jnp.array([-N_GY, N_GY, -1, 1, 0, 0], dtype=jnp.int32)
    never = jnp.zeros((tile_total,), dtype=bool)
    exists = jnp.stack([grid_x > 0, grid_x < N_GX - 1, grid_y > 0, grid_y < N_GY - 1, never, never], axis=1)
    other_device = jnp.clip(device[:, None] + offsets[None, :], 0, N_GX * N_GY - 1)
    other_count = counts[other_device]
    local_code = (slot_index[:, None] + 1 + pick_local % (own_count[:, None] - 1)) % own_count[:, None]
    remote_code = SLOTS + pick_remote % other_count
    face_codes = jnp.where(face_kinds == 0, -1, jnp.where((face_kinds == 2) & exists, remote_code, local_code))
    face_codes = jnp.where((slot_index < own_count)[:, None], face_codes, -1)
    return face_codes.astype(jnp.int32)


def block_scale(own_key, shape, shards, low, largest):
    def one(axis_at, blocks):
        draws = jax.random.uniform(jax.random.fold_in(jax.random.fold_in(own_key, 6), axis_at), (blocks,), jnp.float32, low / len(shards), largest / len(shards))
        return jnp.repeat(jnp.exp(draws), shape[axis_at] // blocks).reshape((-1,) + (1,) * (len(shape) - axis_at - 1))

    factor_of = one(*shards[0])
    for cut in shards[1:]:
        factor_of = factor_of * one(*cut)
    return factor_of


def gaussian(own_key, shape, deviation, most, cuts=(), kind=jnp.bfloat16):
    drawn = jax.random.normal(own_key, shape, jnp.float32) * deviation
    if len(cuts) > 0:
        drawn = block_scale(own_key, shape, cuts, -0.22, 0.18) * drawn
    return jnp.clip(drawn, min=-most, max=most).astype(kind)


def setup_inputs(seed: int = 0) -> dict:
    arg_keys = jax.random.split(jax.random.key(seed), 4)
    level_set = gaussian(arg_keys[0], (ALL_TILES, EDGE, EDGE * EDGE), 2.0, 8.0, ((0, 128),), jnp.float32)
    tile_count = draw_tile_count(jax.random.fold_in(arg_keys[3], 71), 0)
    neighbours = draw_neighbours(jax.random.fold_in(arg_keys[3], 71), 0)
    return {"level_set": level_set, "tile_count": tile_count, "neighbours": neighbours}


weno_eps = 1e-06
pseudo_step = 0.3

def smooth_part(diff_a, diff_b, diff_c, diff_d, diff_e):
    stencil_one = diff_a / 3.0 - 7.0 * diff_b / 6.0 + 11.0 * diff_c / 6.0
    stencil_two = -diff_b / 6.0 + 5.0 * diff_c / 6.0 + diff_d / 3.0
    stencil_three = diff_c / 3.0 + 5.0 * diff_d / 6.0 - diff_e / 6.0
    beta_one = 13.0 / 12.0 * jnp.square(diff_a - 2.0 * diff_b + diff_c) + 0.25 * jnp.square(diff_a - 4.0 * diff_b + 3.0 * diff_c)
    beta_two = 13.0 / 12.0 * jnp.square(diff_b - 2.0 * diff_c + diff_d) + 0.25 * jnp.square(diff_b - diff_d)
    beta_three = 13.0 / 12.0 * jnp.square(diff_c - 2.0 * diff_d + diff_e) + 0.25 * jnp.square(3.0 * diff_c - 4.0 * diff_d + diff_e)
    alpha_one = 0.1 / jnp.square(weno_eps + beta_one)
    alpha_two = 0.6 / jnp.square(weno_eps + beta_two)
    alpha_three = 0.3 / jnp.square(weno_eps + beta_three)
    return (alpha_one * stencil_one + alpha_two * stencil_two + alpha_three * stencil_three) / (alpha_one + alpha_two + alpha_three)

def oriented(tile_flat, direction):
    edge_size = tile_flat.shape[0]
    cube_view = tile_flat.reshape(edge_size, edge_size, edge_size)
    if direction == 1:
        cube_view = jnp.transpose(cube_view, (1, 0, 2))
    elif direction == 2:
        cube_view = jnp.transpose(cube_view, (2, 0, 1))
    return cube_view.reshape(edge_size, edge_size * edge_size)

def restored(turned_flat, direction):
    edge_size = turned_flat.shape[0]
    cube_view = turned_flat.reshape(edge_size, edge_size, edge_size)
    if direction == 1:
        cube_view = jnp.transpose(cube_view, (1, 0, 2))
    elif direction == 2:
        cube_view = jnp.transpose(cube_view, (1, 2, 0))
    return cube_view.reshape(edge_size, edge_size * edge_size)

def face_layers(tile_flat, direction, upper_side):
    turned = oriented(tile_flat, direction)
    edge_size = turned.shape[0]
    if upper_side == 1:
        return turned[edge_size - 3:]
    return turned[:3]

def one_sided(padded):
    diffs = padded[1:] - padded[:-1]
    inner = padded.shape[0] - 6
    parts = [diffs[k:k + inner] for k in range(6)]
    minus_side = smooth_part(parts[0], parts[1], parts[2], parts[3], parts[4])
    plus_side = smooth_part(parts[5], parts[4], parts[3], parts[2], parts[1])
    return (minus_side, plus_side)

def upwind_square(minus_side, plus_side, sign_part):
    outward = jnp.maximum(jnp.square(jnp.maximum(minus_side, 0.0)), jnp.square(jnp.minimum(plus_side, 0.0)))
    inward = jnp.maximum(jnp.square(jnp.minimum(minus_side, 0.0)), jnp.square(jnp.maximum(plus_side, 0.0)))
    return jnp.where(sign_part > 0.0, outward, inward)

def tile_rate(tile_flat, halo_layers, sign_tile):
    squares = jnp.zeros_like(tile_flat)
    for direction in range(3):
        turned = oriented(tile_flat, direction)
        padded = jnp.concatenate([halo_layers[2 * direction], turned, halo_layers[2 * direction + 1]], axis=0)
        minus_side, plus_side = one_sided(padded)
        squares = squares + restored(upwind_square(minus_side, plus_side, oriented(sign_tile, direction)), direction)
    return -sign_tile * (jnp.sqrt(squares) - 1.0)

def reference(level_set, tile_count, neighbours):
    tile_total = level_set.shape[0]
    sign_field = level_set / jnp.sqrt(jnp.square(level_set) + 1.0)
    steps_apart = [-N_GY, N_GY, -1, 1, 0, 0]

    def rates(level_field):

        def per_tile(tile_index):
            device = tile_index // SLOTS
            own_tile = lax.dynamic_index_in_dim(level_field, tile_index, 0, keepdims=False)
            halo_list = []
            for face_index in range(6):
                direction = face_index // 2
                upper_side = face_index % 2
                neighbour_code = neighbours[tile_index, face_index]
                local_target = device * SLOTS + neighbour_code
                remote_target = (device + steps_apart[face_index]) * SLOTS + neighbour_code - SLOTS
                target = jnp.where(neighbour_code < SLOTS, local_target, remote_target)
                target = jnp.clip(target, 0, tile_total - 1).astype(jnp.int32)
                other_tile = lax.dynamic_index_in_dim(level_field, target, 0, keepdims=False)
                face_values = face_layers(other_tile, direction, 1 - upper_side)
                own_face = face_layers(own_tile, direction, upper_side)
                edge_row = own_face[2] if upper_side == 1 else own_face[0]
                border = jnp.broadcast_to(edge_row[None, :], face_values.shape)
                halo_list.append(jnp.where(neighbour_code < 0, border, face_values))
            sign_tile = lax.dynamic_index_in_dim(sign_field, tile_index, 0, keepdims=False)
            return tile_rate(own_tile, jnp.stack(halo_list), sign_tile)
        return lax.map(per_tile, jnp.arange(tile_total, dtype=jnp.int32))
    section_one = level_set + pseudo_step * rates(level_set)
    section_two = 0.75 * level_set + 0.25 * (section_one + pseudo_step * rates(section_one))
    section_three = level_set / 3.0 + 2.0 / 3.0 * (section_two + pseudo_step * rates(section_two))
    tile_ids = jnp.arange(tile_total, dtype=jnp.int32)
    live_mask = tile_ids % SLOTS < tile_count[tile_ids // SLOTS]
    return jnp.where(live_mask[:, None, None], section_three, 0.0)
```

```python
import functools

import jax
import jax.numpy as jnp
from jax import lax
from jax.experimental import pallas as pl
from jax.experimental.pallas import tpu as pltpu
from jax.sharding import PartitionSpec as P

weno_eps = 1e-06
pseudo_step = 0.3
scale_s = pseudo_step / 3.0

SLOTS = 4
EDGE = 64
FACE = SLOTS * 3 * 4


def rcp(x):
    return pl.reciprocal(x, approx=True)


def aligned(start, count=8):
    return pl.ds(pl.multiple_of(start, 8), count)


def column(load, load_s, emit, n):
    kept = {}

    def memo(name, p, make):
        key = (name, p)
        if key not in kept:
            kept[key] = make()
        return kept[key]

    U = lambda p: memo("u", p, lambda: load(p))
    D = lambda p: memo("d", p, lambda: U(p + 1) - U(p))
    E = lambda p: memo("e", p, lambda: D(p) - D(p - 1))
    EH = lambda p: memo("eh", p, lambda: E(p) * 0.5)
    FH = lambda p: memo("fh", p, lambda: EH(p + 1) - EH(p))
    GH = lambda p: memo("gh", p, lambda: FH(p) - FH(p - 1))
    G15 = lambda p: memo("g15", p, lambda: GH(p) * 1.5)
    FF = lambda p: memo("ff", p, lambda: (FH(p) * FH(p)) * (8.0 / 3.0) + 0.5 * weno_eps)
    SQ = lambda p: memo("sq", p, lambda: E(p) * E(p))
    PP = lambda p: memo("pp", p, lambda: E(p) * EH(p + 1))
    LOW = lambda p: memo("low", p, lambda: FF(p) - PP(p))

    def face(j):
        def make():
            ra = rcp(LOW(j - 2) + SQ(j - 1))
            rb = rcp(FF(j - 1) + PP(j - 1))
            c = LOW(j) + SQ(j)
            xr = c * ra
            yr = c * rb
            x = xr * xr
            y = (yr * yr) * 3.0
            w = x * 0.5 + y
            a = x * GH(j - 1)
            minus = (a + G15(j)) * rcp(w + 1.5)
            plus = (GH(j) + a * 1.5) * rcp((w + 0.5) + x)
            return minus, plus

        return memo("face", j, make)

    for i in range(n):
        qm = face(i)[0]
        qp = face(i + 1)[1]
        t = (U(i + 1) - U(i - 1)) + (D(i - 1) + EH(i - 1))
        s = load_s(i)
        w = jnp.maximum(jnp.maximum(s * (t - qm), s * ((GH(i) - t) - qp)), 0.0)
        emit(i, w * w)


def w_row(t, ib, j):
    return ((t * 8 + ib) * 32 + j) * 8


def v_block(t, block, k):
    return (t * 4 + block) * EDGE + k


def face_block(side, t, h, c):
    return ((side * SLOTS + t) * 3 + h) * 4 + c


def one_if_none(n):
    return jnp.maximum(-n, 0)


def one_if_far(n):
    return jnp.minimum(jnp.maximum(n - (SLOTS - 1), 0), 1)


def kernel(
    level_ref, nb_ref, out_ref,
    wa, wb, wc, s_ref, v_ref, sv_ref, gx_ref, gz_ref, gva, gvb,
    x_faces0, x_faces1, x_faces2, y_faces0, y_faces1, y_faces2, send_sem, recv_sem,
):
    v_rows = v_ref.reshape(SLOTS * 4 * EDGE * 8, 128)
    gx, gy = lax.axis_index("gx"), lax.axis_index("gy")
    n_gx, n_gy = lax.axis_size("gx"), lax.axis_size("gy")
    x_low, x_high = lax.rem(gx + n_gx - 1, n_gx), lax.rem(gx + 1, n_gx)
    y_low, y_high = lax.rem(gy + n_gy - 1, n_gy), lax.rem(gy + 1, n_gy)
    lanes_low = lax.broadcasted_iota(jnp.int32, (8, 128), 1) < 64

    def roll(x):
        return pltpu.roll(x, 64, axis=1)

    barrier = pltpu.get_barrier_semaphore()
    around = ((x_low, gy), (x_high, gy), (gx, y_low), (gx, y_high))
    for device in around:
        pl.semaphore_signal(barrier, inc=1, device_id=device, device_id_type=pl.DeviceIdType.MESH)

    def to_v(values, t, ib, half):
        turned = jnp.concatenate(values, axis=0).T
        for jh in range(2):
            line = lax.rem(ib, 2) * 4 + half * 2 + jh
            for m in range(8):
                r = jh * 64 + 8 * m
                start = v_block(t, ib // 2, 8 * m) * 8 + line
                v_rows[pl.ds(start, 8, stride=8), :] = turned[r:r + 8]

    def enter(it, carry):
        t, ib = it // 8, lax.rem(it, 8)
        rows = aligned(ib * 8)
        values = []
        for m in range(16):
            a = level_ref[t, rows, m * 128:(m + 1) * 128]
            b = level_ref[t, rows, (m + 16) * 128:(m + 17) * 128]
            values.append(jnp.where(lanes_low, a, roll(b)))
            values.append(jnp.where(lanes_low, roll(a), b))
        for j in range(32):
            u = values[j]
            wa[aligned(w_row(t, ib, j)), :] = u
            s_ref[aligned(w_row(t, ib, j)), :] = (u * scale_s) * lax.rsqrt(u * u + 1.0)
        for half in range(2):
            to_v(values[16 * half:16 * half + 16], t, ib, half)
        return carry

    lax.fori_loop(0, 32, enter, 0)

    def turned_sign(it, carry):
        for k in range(64):
            u = v_ref[it * 64 + k]
            sv_ref[it * 64 + k] = (u * scale_s) * lax.rsqrt(u * u + 1.0)
        return carry

    lax.fori_loop(0, 16, turned_sign, 0)
    gvb[...] = jnp.zeros_like(gvb)
    pl.semaphore_wait(barrier, 4)

    def section(stage, u_ref, n_ref, xf, yf):
        def pack(t, carry):
            for side in range(2):
                for h in range(3):
                    i = h if side == 0 else 61 + h
                    for c in range(4):
                        rows = pl.ds(w_row(t, i // 8, 8 * c) + i % 8, 8, stride=8)
                        xf[face_block(side, t, h, c)] = u_ref[rows, :]
                    for q in range(4):
                        j = h if side == 0 else 29 + h
                        even = u_ref[aligned(w_row(t, 2 * q, j)), :]
                        odd = u_ref[aligned(w_row(t, 2 * q + 1, j)), :]
                        if side == 0:
                            both = jnp.where(lanes_low, even, roll(odd))
                        else:
                            both = jnp.where(lanes_low, roll(even), odd)
                        yf[face_block(side, t, h, q)] = both
            return carry

        lax.fori_loop(0, 4, pack, 0)
        low, high, below, above = (pl.ds(part * FACE, FACE) for part in range(4))
        plan = (
            (xf, high, below, (x_high, gy)), (xf, low, above, (x_low, gy)),
            (yf, high, below, (gx, y_high)), (yf, low, above, (gx, y_low)),
        )
        copies = []
        for f, (table, source, target, device) in enumerate(plan):
            copy = pltpu.make_async_remote_copy(
                src_ref=table.at[source], dst_ref=table.at[target], send_sem=send_sem.at[stage, f],
                recv_sem=recv_sem.at[stage, f], device_id=device, device_id_type=pl.DeviceIdType.MESH,
            )
            copy.start()
            copies.append(copy)

        def z_back(source, it):
            for pair in range(4):
                parts = [
                    source[pl.ds(64 * m + 2 * pair + jh, 8, stride=8), :] for jh in range(2) for m in range(8)
                ]
                gz_ref[aligned(512 + it * 512 + pair * 128, 128), :] = jnp.concatenate(parts, axis=0).T

        def z_stream(it, target):
            t, block = it // 4, lax.rem(it, 4)
            base = v_block(t, block, 0)

            def layer(n, own, other):
                none = one_if_none(n)
                return none * (t * 256 + own) + (1 - none) * (n * 256 + other) + block * EDGE

            n_low, n_high = nb_ref[t, 4], nb_ref[t, 5]

            def load(p):
                if p < 0:
                    return v_ref[layer(n_low, 0, 64 + p)]
                if p >= 64:
                    return v_ref[layer(n_high, 63, p - 64)]
                return v_ref[base + p]

            def emit(i, squares):
                target[pl.ds(i * 8, 8), :] = squares

            column(load, lambda i: sv_ref[base + i], emit, 64)

        def z_pair(n, carry):
            z_back(gvb, 2 * n - 1)
            z_stream(2 * n, gva)
            z_back(gva, 2 * n)
            z_stream(2 * n + 1, gvb)
            return carry

        lax.fori_loop(0, 8, z_pair, 0)
        z_back(gvb, 15)

        for copy in copies:
            copy.wait()

        def face_source(t, f, table):
            n = nb_ref[t, f]
            own_side, other_side = (0, 1) if f % 2 == 0 else (1, 0)
            outer = 0 if f % 2 == 0 else 2
            none, far = one_if_none(n), one_if_far(n)
            own = none * face_block(own_side, t, outer, 0)
            near = (1 - none) * (1 - far) * face_block(other_side, n, 0, 0)
            away = far * ((2 + f % 2) * FACE + (n - SLOTS) * 12)

            def get(h, c):
                return table[own + near + away + (1 - none) * (4 * h) + c]

            return get

        def x_stream(it, carry):
            t, c = it // 4, lax.rem(it, 4)
            get_low = face_source(t, 0, xf)
            get_high = face_source(t, 1, xf)

            def rows(i):
                return pl.ds(w_row(t, i // 8, 8 * c) + i % 8, 8, stride=8)

            def load(p):
                if p < 0:
                    return get_low(p + 3, c)
                if p >= 64:
                    return get_high(p - 64, c)
                return u_ref[rows(p), :]

            def emit(i, squares):
                gx_ref[rows(i), :] = squares

            column(load, lambda i: s_ref[rows(i), :], emit, 64)
            return carry

        lax.fori_loop(0, 16, x_stream, 0)

        def y_stream(t, q, parity, lows, highs):
            ib = 2 * q + parity
            base = w_row(t, ib, 0)
            new = {}

            def load(p):
                if p < 0:
                    h = p + 3
                    halo = lows[h] if parity == 0 else roll(lows[h])
                    return jnp.where(lanes_low, halo, roll(u_ref[aligned(base + (29 + h) * 8), :]))
                if p >= 32:
                    h = p - 32
                    halo = roll(highs[h]) if parity == 0 else highs[h]
                    return jnp.where(lanes_low, roll(u_ref[aligned(base + h * 8), :]), halo)
                return u_ref[aligned(base + p * 8), :]

            def emit(j, squares):
                rows = aligned(base + j * 8)
                total = (squares + gx_ref[rows, :]) + gz_ref[aligned(512 + base + j * 8), :]
                size = total * lax.rsqrt(jnp.maximum(total, 1e-35))
                s = s_ref[rows, :]
                u = u_ref[rows, :]
                moved = u + s * 3.0
                moved = jnp.where(s > 0.0, moved - size, moved + size)
                if stage == 1:
                    moved = 0.75 * wa[rows, :] + 0.25 * moved
                elif stage == 2:
                    moved = (1.0 / 3.0) * wa[rows, :] + (2.0 / 3.0) * moved
                if stage < 2:
                    n_ref[rows, :] = moved
                new[j] = moved
                if stage == 2 and j % 2 == 1:
                    a, b = new[j - 1], moved
                    m = j // 2
                    orow = aligned(ib * 8)
                    out_ref[t, orow, m * 128:(m + 1) * 128] = jnp.where(lanes_low, a, roll(b))
                    out_ref[t, orow, (m + 16) * 128:(m + 17) * 128] = jnp.where(lanes_low, roll(a), b)

            column(load, lambda j: s_ref[aligned(base + j * 8), :], emit, 32)
            return [new[j] for j in range(32)]

        def y_pair(it, carry):
            t, q = it // 4, lax.rem(it, 4)
            get_low = face_source(t, 2, yf)
            get_high = face_source(t, 3, yf)
            lows = [get_low(h, q) for h in range(3)]
            highs = [get_high(h, q) for h in range(3)]
            for parity in range(2):
                values = y_stream(t, q, parity, lows, highs)
                if stage < 2:
                    for half in range(2):
                        to_v(values[16 * half:16 * half + 16], t, 2 * q + parity, half)
            return carry

        lax.fori_loop(0, 16, y_pair, 0)

    section(0, wa, wb, x_faces0, y_faces0)
    section(1, wb, wc, x_faces1, y_faces1)
    section(2, wc, None, x_faces2, y_faces2)


def local(level_set, tile_count, neighbours):
    rows = lambda count: pltpu.VMEM((count, 128), jnp.float32)
    blocks = lambda count: pltpu.VMEM((count, 8, 128), jnp.float32)
    whole = SLOTS * EDGE ** 3 // 128
    scratch = [rows(whole), rows(whole), rows(whole), rows(whole), blocks(whole // 8), blocks(whole // 8),
               rows(whole), rows(whole + 512), rows(512), rows(512)]
    scratch += [blocks(4 * FACE) for _ in range(6)]
    scratch += [pltpu.SemaphoreType.DMA((3, 4)), pltpu.SemaphoreType.DMA((3, 4))]
    cells = SLOTS * EDGE ** 3
    moved = pl.pallas_call(
        kernel,
        out_shape=jax.ShapeDtypeStruct(level_set.shape, jnp.float32),
        in_specs=[
            pl.BlockSpec(memory_space=pltpu.VMEM),
            pl.BlockSpec(memory_space=pltpu.SMEM),
        ],
        out_specs=pl.BlockSpec(memory_space=pltpu.VMEM),
        scratch_shapes=scratch,
        compiler_params=pltpu.CompilerParams(
            collective_id=0, has_side_effects=True, vmem_limit_bytes=60 * 2 ** 20
        ),
        cost_estimate=pl.CostEstimate(flops=cells * 3 * 150, bytes_accessed=cells * 8, transcendentals=cells * 3),
    )(level_set, neighbours)
    live = jnp.arange(SLOTS, dtype=jnp.int32) < tile_count[0]
    return jnp.where(live[:, None, None], moved, 0.0)


def solution(mesh):
    placed = (P(("gx", "gy"), None, None), P(("gx", "gy")), P(("gx", "gy"), None))
    return jax.shard_map(
        local, mesh=mesh, in_specs=placed, out_specs=P(("gx", "gy"), None, None), check_vma=False
    )
```

```python
import functools

import jax
import jax.numpy as jnp
from jax import lax
from jax.experimental import pallas as pl
from jax.experimental.pallas import tpu as pltpu
from jax.sharding import PartitionSpec as P

weno_eps = 1e-06
pseudo_step = 0.3
scale_s = pseudo_step / 3.0

SLOTS = 4
EDGE = 64
FACE = SLOTS * 3 * 4


def rcp(x):
    return pl.reciprocal(x, approx=True)


def aligned(start, count=8):
    return pl.ds(pl.multiple_of(start, 8), count)


def column(load, load_s, emit, n, between=None):
    kept = {}

    def memo(name, p, make):
        key = (name, p)
        if key not in kept:
            kept[key] = make()
        return kept[key]

    U = lambda p: memo("u", p, lambda: load(p))
    D = lambda p: memo("d", p, lambda: U(p + 1) - U(p))
    E = lambda p: memo("e", p, lambda: D(p) - D(p - 1))
    EH = lambda p: memo("eh", p, lambda: E(p) * 0.5)
    FH = lambda p: memo("fh", p, lambda: EH(p + 1) - EH(p))
    GH = lambda p: memo("gh", p, lambda: FH(p) - FH(p - 1))
    G15 = lambda p: memo("g15", p, lambda: GH(p) * 1.5)
    FF = lambda p: memo("ff", p, lambda: (FH(p) * FH(p)) * (8.0 / 3.0) + 0.5 * weno_eps)
    SQ = lambda p: memo("sq", p, lambda: E(p) * E(p))
    PP = lambda p: memo("pp", p, lambda: E(p) * EH(p + 1))
    LOW = lambda p: memo("low", p, lambda: FF(p) - PP(p))

    def face(j):
        def make():
            ra = rcp(LOW(j - 2) + SQ(j - 1))
            rb = rcp(FF(j - 1) + PP(j - 1))
            c = LOW(j) + SQ(j)
            xr = c * ra
            yr = c * rb
            x = xr * xr
            y = (yr * yr) * 3.0
            w = x * 0.5 + y
            a = x * GH(j - 1)
            minus = (a + G15(j)) * rcp(w + 1.5)
            plus = (GH(j) + a * 1.5) * rcp((w + 0.5) + x)
            return minus, plus

        return memo("face", j, make)

    for i in range(n):
        qm = face(i)[0]
        qp = face(i + 1)[1]
        t = (U(i + 1) - U(i - 1)) + (D(i - 1) + EH(i - 1))
        s = load_s(i)
        w = jnp.maximum(jnp.maximum(s * (t - qm), s * ((GH(i) - t) - qp)), 0.0)
        emit(i, w * w)
        if between is not None:
            between(i)


def w_row(t, ib, j):
    return ((t * 8 + ib) * 32 + j) * 8


def v_block(t, block, k):
    return (t * 4 + block) * EDGE + k


def face_block(side, t, h, c):
    return ((side * SLOTS + t) * 3 + h) * 4 + c


def one_if_none(n):
    return jnp.maximum(-n, 0)


def one_if_far(n):
    return jnp.minimum(jnp.maximum(n - (SLOTS - 1), 0), 1)


def kernel(
    level_ref, nb_ref, out_ref,
    wa, wb, wc, s_ref, ux_ref, sx_ref, v_ref, sv_ref, gx_ref, gz_ref, gva, gvb,
    x_faces0, x_faces1, x_faces2, y_faces0, y_faces1, y_faces2, send_sem, recv_sem, load_sem,
):
    v_rows = v_ref.reshape(SLOTS * 4 * EDGE * 8, 128)
    ux_rows = ux_ref.reshape(SLOTS * 4 * EDGE * 8, 128)
    sx_rows = sx_ref.reshape(SLOTS * 4 * EDGE * 8, 128)

    def x_rows(t, ib, j):
        return pl.ds(v_block(t, j // 8, ib * 8) * 8 + j % 8, 8, stride=8)
    gx, gy = lax.axis_index("gx"), lax.axis_index("gy")
    n_gx, n_gy = lax.axis_size("gx"), lax.axis_size("gy")
    x_low, x_high = lax.rem(gx + n_gx - 1, n_gx), lax.rem(gx + 1, n_gx)
    y_low, y_high = lax.rem(gy + n_gy - 1, n_gy), lax.rem(gy + 1, n_gy)
    lanes_low = lax.broadcasted_iota(jnp.int32, (8, 128), 1) < 64

    def roll(x):
        return pltpu.roll(x, 64, axis=1)

    tile_rows = [pl.ds(t * 2048, 2048) for t in range(SLOTS)]
    loads = [pltpu.make_async_copy(level_ref.at[r], wc.at[r], load_sem.at[t]) for t, r in enumerate(tile_rows)]
    for load in loads:
        load.start()

    barrier = pltpu.get_barrier_semaphore()
    around = ((x_low, gy), (x_high, gy), (gx, y_low), (gx, y_high))
    for device in around:
        pl.semaphore_signal(barrier, inc=1, device_id=device, device_id_type=pl.DeviceIdType.MESH)

    def to_v(values, t, ib, half):
        turned = jnp.concatenate(values, axis=0).T
        for jh in range(2):
            line = lax.rem(ib, 2) * 4 + half * 2 + jh
            for m in range(8):
                r = jh * 64 + 8 * m
                start = v_block(t, ib // 2, 8 * m) * 8 + line
                v_rows[pl.ds(start, 8, stride=8), :] = turned[r:r + 8]

    def enter_block(t, ib):
        values = []
        for m in range(16):
            a = wc[aligned(w_row(t, ib, m)), :]
            b = wc[aligned(w_row(t, ib, m + 16)), :]
            values.append(jnp.where(lanes_low, a, roll(b)))
            values.append(jnp.where(lanes_low, roll(a), b))
        for j in range(32):
            u = values[j]
            wa[aligned(w_row(t, ib, j)), :] = u
            s = (u * scale_s) * lax.rsqrt(u * u + 1.0)
            s_ref[aligned(w_row(t, ib, j)), :] = s
            ux_rows[x_rows(t, ib, j), :] = u
            sx_rows[x_rows(t, ib, j), :] = s
        for half in range(2):
            to_v(values[16 * half:16 * half + 16], t, ib, half)

    for t in range(SLOTS):
        def enter(q, carry, t=t):
            for e in range(2):
                enter_block(t, 2 * q + e)
            return carry

        loads[t].wait()
        lax.fori_loop(0, 4, enter, 0)

    def turned_sign(it, carry):
        for k in range(64):
            u = v_ref[it * 64 + k]
            sv_ref[it * 64 + k] = (u * scale_s) * lax.rsqrt(u * u + 1.0)
        return carry

    lax.fori_loop(0, 16, turned_sign, 0)
    gvb[...] = jnp.zeros_like(gvb)
    pl.semaphore_wait(barrier, 4)

    def section(stage, u_ref, n_ref, xf, yf):
        def pack(t, carry):
            for side in range(2):
                for h in range(3):
                    i = h if side == 0 else 61 + h
                    for c in range(4):
                        xf[face_block(side, t, h, c)] = ux_ref[v_block(t, c, i)]
                    for q in range(4):
                        j = h if side == 0 else 29 + h
                        even = u_ref[aligned(w_row(t, 2 * q, j)), :]
                        odd = u_ref[aligned(w_row(t, 2 * q + 1, j)), :]
                        if side == 0:
                            both = jnp.where(lanes_low, even, roll(odd))
                        else:
                            both = jnp.where(lanes_low, roll(even), odd)
                        yf[face_block(side, t, h, q)] = both
            return carry

        lax.fori_loop(0, 4, pack, 0)
        low, high, below, above = (pl.ds(part * FACE, FACE) for part in range(4))
        plan = (
            (xf, high, below, (x_high, gy)), (xf, low, above, (x_low, gy)),
            (yf, high, below, (gx, y_high)), (yf, low, above, (gx, y_low)),
        )
        copies = []
        for f, (table, source, target, device) in enumerate(plan):
            copy = pltpu.make_async_remote_copy(
                src_ref=table.at[source], dst_ref=table.at[target], send_sem=send_sem.at[stage, f],
                recv_sem=recv_sem.at[stage, f], device_id=device, device_id_type=pl.DeviceIdType.MESH,
            )
            copy.start()
            copies.append(copy)

        def z_back(source, it, pair):
            parts = [source[pl.ds((8 * m + 2 * pair + jh) * 8, 8), :] for jh in range(2) for m in range(8)]
            gz_ref[aligned(512 + it * 512 + pair * 128, 128), :] = jnp.concatenate(parts, axis=0).T

        def z_stream(it, target, before):
            t, block = it // 4, lax.rem(it, 4)
            base = v_block(t, block, 0)

            def layer(n, own, other):
                none = one_if_none(n)
                return none * (t * 256 + own) + (1 - none) * (n * 256 + other) + block * EDGE

            n_low, n_high = nb_ref[t, 4], nb_ref[t, 5]

            def load(p):
                if p < 0:
                    return v_ref[layer(n_low, 0, 64 + p)]
                if p >= 64:
                    return v_ref[layer(n_high, 63, p - 64)]
                return v_ref[base + p]

            def emit(i, squares):
                target[pl.ds((i // 8) * 64 + i % 8, 8, stride=8), :] = squares

            def between(i):
                if i % 16 == 4:
                    z_back(before, it - 1, i // 16)

            column(load, lambda i: sv_ref[base + i], emit, 64, between)

        def z_pair(n, carry):
            z_stream(2 * n, gva, gvb)
            z_stream(2 * n + 1, gvb, gva)
            return carry

        lax.fori_loop(0, 8, z_pair, 0)
        for pair in range(4):
            z_back(gvb, 15, pair)

        for copy in copies:
            copy.wait()

        def face_source(t, f, table):
            n = nb_ref[t, f]
            own_side, other_side = (0, 1) if f % 2 == 0 else (1, 0)
            outer = 0 if f % 2 == 0 else 2
            none, far = one_if_none(n), one_if_far(n)
            own = none * face_block(own_side, t, outer, 0)
            near = (1 - none) * (1 - far) * face_block(other_side, n, 0, 0)
            away = far * ((2 + f % 2) * FACE + (n - SLOTS) * 12)

            def get(h, c):
                return table[own + near + away + (1 - none) * (4 * h) + c]

            return get

        def x_stream(t, c):
            get_low = face_source(t, 0, xf)
            get_high = face_source(t, 1, xf)

            base = v_block(t, c, 0)

            def load(p):
                if p < 0:
                    return get_low(p + 3, c)
                if p >= 64:
                    return get_high(p - 64, c)
                return ux_ref[base + p]

            def emit(i, squares):
                gx_ref[pl.ds(w_row(0, i // 8, 8 * c) + i % 8, 8, stride=8), :] = squares

            column(load, lambda i: sx_ref[base + i], emit, 64)

        def y_stream(t, q, parity, lows, highs, between):
            ib = 2 * q + parity
            base = w_row(t, ib, 0)
            new = {}

            def load(p):
                if p < 0:
                    h = p + 3
                    halo = lows[h] if parity == 0 else roll(lows[h])
                    return jnp.where(lanes_low, halo, roll(u_ref[aligned(base + (29 + h) * 8), :]))
                if p >= 32:
                    h = p - 32
                    halo = roll(highs[h]) if parity == 0 else highs[h]
                    return jnp.where(lanes_low, roll(u_ref[aligned(base + h * 8), :]), halo)
                return u_ref[aligned(base + p * 8), :]

            def emit(j, squares):
                rows = aligned(base + j * 8)
                total = (squares + gx_ref[aligned(w_row(0, ib, j)), :]) + gz_ref[aligned(512 + base + j * 8), :]
                size = total * lax.rsqrt(jnp.maximum(total, 1e-35))
                s = s_ref[rows, :]
                u = u_ref[rows, :]
                moved = u + s * 3.0
                moved = jnp.where(s > 0.0, moved - size, moved + size)
                if stage == 1:
                    moved = 0.75 * wa[rows, :] + 0.25 * moved
                elif stage == 2:
                    moved = (1.0 / 3.0) * wa[rows, :] + (2.0 / 3.0) * moved
                if stage < 2:
                    n_ref[rows, :] = moved
                    ux_rows[x_rows(t, ib, j), :] = moved
                new[j] = moved
                if stage == 2 and j % 2 == 1:
                    a, b = new[j - 1], moved
                    m = j // 2
                    orow = aligned(ib * 8)
                    out_ref[t, orow, m * 128:(m + 1) * 128] = jnp.where(lanes_low, a, roll(b))
                    out_ref[t, orow, (m + 16) * 128:(m + 17) * 128] = jnp.where(lanes_low, roll(a), b)

            column(load, lambda j: s_ref[aligned(base + j * 8), :], emit, 32, between)

        def y_pair(t, q):
            it = t * 4 + q
            get_low = face_source(t, 2, yf)
            get_high = face_source(t, 3, yf)
            lows = [get_low(h, q) for h in range(3)]
            highs = [get_high(h, q) for h in range(3)]
            before = jnp.maximum(it - 1, 0)
            y_stream(t, q, 0, lows, highs, functools.partial(turn, before // 4, 2 * lax.rem(before, 4) + 1))
            y_stream(t, q, 1, lows, highs, functools.partial(turn, t, 2 * q))

        def turn(t, ib, j):
            if stage < 2 and j % 16 == 4:
                half = j // 16
                to_v([n_ref[aligned(w_row(t, ib, 16 * half + k)), :] for k in range(16)], t, ib, half)

        def tile(t, carry):
            lax.fori_loop(0, 4, lambda c, kept: (x_stream(t, c), kept)[1], 0)
            lax.fori_loop(0, 4, lambda q, kept: (y_pair(t, q), kept)[1], 0)
            return carry

        lax.fori_loop(0, SLOTS, tile, 0)
        for j in (4, 20):
            turn(3, 7, j)

    section(0, wa, wb, x_faces0, y_faces0)
    section(1, wb, wc, x_faces1, y_faces1)
    section(2, wc, None, x_faces2, y_faces2)


def local(level_set, tile_count, neighbours):
    rows = lambda count: pltpu.VMEM((count, 128), jnp.float32)
    blocks = lambda count: pltpu.VMEM((count, 8, 128), jnp.float32)
    whole = SLOTS * EDGE ** 3 // 128
    scratch = [rows(whole), rows(whole), rows(whole), rows(whole), blocks(whole // 8), blocks(whole // 8),
               blocks(whole // 8), blocks(whole // 8),
               rows(whole // SLOTS), rows(whole + 512), rows(512), rows(512)]
    scratch += [blocks(4 * FACE) for _ in range(6)]
    scratch += [pltpu.SemaphoreType.DMA((3, 4)), pltpu.SemaphoreType.DMA((3, 4)), pltpu.SemaphoreType.DMA((SLOTS,))]
    cells = SLOTS * EDGE ** 3
    blocked = level_set.reshape(SLOTS, 8, 8, 32, 128).transpose(0, 1, 3, 2, 4).reshape(whole, 128)
    moved = pl.pallas_call(
        kernel,
        out_shape=jax.ShapeDtypeStruct(level_set.shape, jnp.float32),
        in_specs=[
            pl.BlockSpec(memory_space=pl.ANY),
            pl.BlockSpec(memory_space=pltpu.SMEM),
        ],
        out_specs=pl.BlockSpec(memory_space=pltpu.VMEM),
        scratch_shapes=scratch,
        compiler_params=pltpu.CompilerParams(
            collective_id=0, has_side_effects=True, vmem_limit_bytes=47 * 2 ** 20
        ),
        cost_estimate=pl.CostEstimate(flops=cells * 3 * 150, bytes_accessed=cells * 8, transcendentals=cells * 3),
    )(blocked, neighbours)
    live = jnp.arange(SLOTS, dtype=jnp.int32) < tile_count[0]
    return jnp.where(live[:, None, None], moved, 0.0)


def solution(mesh):
    placed = (P(("gx", "gy"), None, None), P(("gx", "gy")), P(("gx", "gy"), None))
    return jax.shard_map(
        local, mesh=mesh, in_specs=placed, out_specs=P(("gx", "gy"), None, None), check_vma=False
    )
```

```python
import functools

import jax
import jax.numpy as jnp
from jax import lax
from jax.experimental import pallas as pl
from jax.experimental.pallas import tpu as pltpu
from jax.sharding import PartitionSpec as P

weno_eps = 1e-06
pseudo_step = 0.3
scale_s = pseudo_step / 3.0

SLOTS = 4
EDGE = 64
FACE = SLOTS * 3 * 4


def rcp(x):
    return pl.reciprocal(x, approx=True)


def aligned(start, count=8):
    return pl.ds(pl.multiple_of(start, 8), count)


def column(load, load_s, emit, n, between=None):
    kept = {}

    def memo(name, p, make):
        key = (name, p)
        if key not in kept:
            kept[key] = make()
        return kept[key]

    U = lambda p: memo("u", p, lambda: load(p))
    D = lambda p: memo("d", p, lambda: U(p + 1) - U(p))
    E = lambda p: memo("e", p, lambda: D(p) - D(p - 1))
    EH = lambda p: memo("eh", p, lambda: E(p) * 0.5)
    FH = lambda p: memo("fh", p, lambda: EH(p + 1) - EH(p))
    GH = lambda p: memo("gh", p, lambda: FH(p) - FH(p - 1))
    G15 = lambda p: memo("g15", p, lambda: GH(p) * 1.5)
    FF = lambda p: memo("ff", p, lambda: (FH(p) * FH(p)) * (8.0 / 3.0) + 0.5 * weno_eps)
    SQ = lambda p: memo("sq", p, lambda: E(p) * E(p))
    PP = lambda p: memo("pp", p, lambda: E(p) * EH(p + 1))
    LOW = lambda p: memo("low", p, lambda: FF(p) - PP(p))

    def face(j):
        def make():
            ra = rcp(LOW(j - 2) + SQ(j - 1))
            rb = rcp(FF(j - 1) + PP(j - 1))
            c = LOW(j) + SQ(j)
            xr = c * ra
            yr = c * rb
            x = xr * xr
            y = (yr * yr) * 3.0
            w = x * 0.5 + y
            a = x * GH(j - 1)
            minus = (a + G15(j)) * rcp(w + 1.5)
            plus = (GH(j) + a * 1.5) * rcp((w + 0.5) + x)
            return minus, plus

        return memo("face", j, make)

    for i in range(n):
        qm = face(i)[0]
        qp = face(i + 1)[1]
        t = (U(i + 1) - U(i - 1)) + (D(i - 1) + EH(i - 1))
        s = load_s(i)
        w = jnp.maximum(jnp.maximum(s * (t - qm), s * ((GH(i) - t) - qp)), 0.0)
        emit(i, w * w, U(i), s)
        if between is not None:
            between(i)


def w_row(t, ib, j):
    return ((t * 8 + ib) * 32 + j) * 8


def v_block(t, block, k):
    return (t * 4 + block) * EDGE + k


def face_block(side, t, h, c):
    return ((side * SLOTS + t) * 3 + h) * 4 + c


def one_if_none(n):
    return jnp.maximum(-n, 0)


def one_if_far(n):
    return jnp.minimum(jnp.maximum(n - (SLOTS - 1), 0), 1)


def kernel(
    level_ref, nb_ref, out_ref,
    wa, wb, wc, s_ref, ux_ref, sx_ref, v_ref, sv_ref, gx_ref, gz_ref, gva, gvb,
    x_faces0, x_faces1, x_faces2, y_faces0, y_faces1, y_faces2, send_sem, recv_sem, load_sem,
):
    v_rows = v_ref.reshape(SLOTS * 4 * EDGE * 8, 128)
    ux_rows = ux_ref.reshape(SLOTS * 4 * EDGE * 8, 128)
    sx_rows = sx_ref.reshape(SLOTS * 4 * EDGE * 8, 128)

    def x_rows(t, ib, j):
        return pl.ds(v_block(t, j // 8, ib * 8) * 8 + j % 8, 8, stride=8)
    gx, gy = lax.axis_index("gx"), lax.axis_index("gy")
    n_gx, n_gy = lax.axis_size("gx"), lax.axis_size("gy")
    x_low, x_high = lax.rem(gx + n_gx - 1, n_gx), lax.rem(gx + 1, n_gx)
    y_low, y_high = lax.rem(gy + n_gy - 1, n_gy), lax.rem(gy + 1, n_gy)
    lanes_low = lax.broadcasted_iota(jnp.int32, (8, 128), 1) < 64

    def roll(x):
        return pltpu.roll(x, 64, axis=1)

    tile_rows = [pl.ds(t * 2048, 2048) for t in range(SLOTS)]
    loads = [pltpu.make_async_copy(level_ref.at[r], wc.at[r], load_sem.at[t]) for t, r in enumerate(tile_rows)]
    for load in loads:
        load.start()

    barrier = pltpu.get_barrier_semaphore()
    around = ((x_low, gy), (x_high, gy), (gx, y_low), (gx, y_high))
    for device in around:
        pl.semaphore_signal(barrier, inc=1, device_id=device, device_id_type=pl.DeviceIdType.MESH)

    def to_v(values, t, ib, half):
        turned = jnp.concatenate(values, axis=0).T
        for jh in range(2):
            line = lax.rem(ib, 2) * 4 + half * 2 + jh
            for m in range(8):
                r = jh * 64 + 8 * m
                start = v_block(t, ib // 2, 8 * m) * 8 + line
                v_rows[pl.ds(start, 8, stride=8), :] = turned[r:r + 8]

    def enter_block(t, ib):
        values = []
        for m in range(16):
            a = wc[aligned(w_row(t, ib, m)), :]
            b = wc[aligned(w_row(t, ib, m + 16)), :]
            values.append(jnp.where(lanes_low, a, roll(b)))
            values.append(jnp.where(lanes_low, roll(a), b))
        for j in range(32):
            u = values[j]
            wa[aligned(w_row(t, ib, j)), :] = u
            s = (u * scale_s) * lax.rsqrt(u * u + 1.0)
            s_ref[aligned(w_row(t, ib, j)), :] = s
            ux_rows[x_rows(t, ib, j), :] = u
            sx_rows[x_rows(t, ib, j), :] = s
        for half in range(2):
            to_v(values[16 * half:16 * half + 16], t, ib, half)

    for t in range(SLOTS):
        def enter(q, carry, t=t):
            for e in range(2):
                enter_block(t, 2 * q + e)
            return carry

        loads[t].wait()
        lax.fori_loop(0, 4, enter, 0)

    def turned_sign(it, carry):
        for k in range(64):
            u = v_ref[it * 64 + k]
            sv_ref[it * 64 + k] = (u * scale_s) * lax.rsqrt(u * u + 1.0)
        return carry

    lax.fori_loop(0, 16, turned_sign, 0)
    gvb[...] = jnp.zeros_like(gvb)
    pl.semaphore_wait(barrier, 4)

    def section(stage, u_ref, n_ref, xf, yf):
        def pack(t, carry):
            for side in range(2):
                for h in range(3):
                    i = h if side == 0 else 61 + h
                    for c in range(4):
                        xf[face_block(side, t, h, c)] = ux_ref[v_block(t, c, i)]
                    for q in range(4):
                        j = h if side == 0 else 29 + h
                        even = u_ref[aligned(w_row(t, 2 * q, j)), :]
                        odd = u_ref[aligned(w_row(t, 2 * q + 1, j)), :]
                        if side == 0:
                            both = jnp.where(lanes_low, even, roll(odd))
                        else:
                            both = jnp.where(lanes_low, roll(even), odd)
                        yf[face_block(side, t, h, q)] = both
            return carry

        lax.fori_loop(0, 4, pack, 0)
        low, high, below, above = (pl.ds(part * FACE, FACE) for part in range(4))
        plan = (
            (xf, high, below, (x_high, gy)), (xf, low, above, (x_low, gy)),
            (yf, high, below, (gx, y_high)), (yf, low, above, (gx, y_low)),
        )
        copies = []
        for f, (table, source, target, device) in enumerate(plan):
            copy = pltpu.make_async_remote_copy(
                src_ref=table.at[source], dst_ref=table.at[target], send_sem=send_sem.at[stage, f],
                recv_sem=recv_sem.at[stage, f], device_id=device, device_id_type=pl.DeviceIdType.MESH,
            )
            copy.start()
            copies.append(copy)

        def z_back(source, it, pair):
            parts = [source[pl.ds((8 * m + 2 * pair + jh) * 8, 8), :] for jh in range(2) for m in range(8)]
            gz_ref[aligned(512 + it * 512 + pair * 128, 128), :] = jnp.concatenate(parts, axis=0).T

        def z_stream(it, target, before):
            t, block = it // 4, lax.rem(it, 4)
            base = v_block(t, block, 0)

            def layer(n, own, other):
                none = one_if_none(n)
                return none * (t * 256 + own) + (1 - none) * (n * 256 + other) + block * EDGE

            n_low, n_high = nb_ref[t, 4], nb_ref[t, 5]

            def load(p):
                if p < 0:
                    return v_ref[layer(n_low, 0, 64 + p)]
                if p >= 64:
                    return v_ref[layer(n_high, 63, p - 64)]
                return v_ref[base + p]

            def emit(i, squares, u, s):
                target[pl.ds((i // 8) * 64 + i % 8, 8, stride=8), :] = squares

            def between(i):
                if i % 16 == 4:
                    z_back(before, it - 1, i // 16)

            column(load, lambda i: sv_ref[base + i], emit, 64, between)

        def z_pair(n, carry):
            z_stream(2 * n, gva, gvb)
            z_stream(2 * n + 1, gvb, gva)
            return carry

        lax.fori_loop(0, 8, z_pair, 0)
        for pair in range(4):
            z_back(gvb, 15, pair)

        for copy in copies:
            copy.wait()

        def face_source(t, f, table):
            n = nb_ref[t, f]
            own_side, other_side = (0, 1) if f % 2 == 0 else (1, 0)
            outer = 0 if f % 2 == 0 else 2
            none, far = one_if_none(n), one_if_far(n)
            own = none * face_block(own_side, t, outer, 0)
            near = (1 - none) * (1 - far) * face_block(other_side, n, 0, 0)
            away = far * ((2 + f % 2) * FACE + (n - SLOTS) * 12)

            def get(h, c):
                return table[own + near + away + (1 - none) * (4 * h) + c]

            return get

        def x_stream(t, c):
            get_low = face_source(t, 0, xf)
            get_high = face_source(t, 1, xf)

            base = v_block(t, c, 0)

            def load(p):
                if p < 0:
                    return get_low(p + 3, c)
                if p >= 64:
                    return get_high(p - 64, c)
                return ux_ref[base + p]

            def emit(i, squares, u, s):
                gx_ref[pl.ds(w_row(0, i // 8, 8 * c) + i % 8, 8, stride=8), :] = squares

            column(load, lambda i: sx_ref[base + i], emit, 64)

        def x_pair(n, t):
            x_stream(t, 2 * n)
            x_stream(t, 2 * n + 1)
            return t

        def y_stream(t, q, parity, lows, highs, between):
            ib = 2 * q + parity
            base = w_row(t, ib, 0)
            new = {}

            def load(p):
                if p < 0:
                    h = p + 3
                    halo = lows[h] if parity == 0 else roll(lows[h])
                    return jnp.where(lanes_low, halo, roll(u_ref[aligned(base + (29 + h) * 8), :]))
                if p >= 32:
                    h = p - 32
                    halo = roll(highs[h]) if parity == 0 else highs[h]
                    return jnp.where(lanes_low, roll(u_ref[aligned(base + h * 8), :]), halo)
                return u_ref[aligned(base + p * 8), :]

            def emit(j, squares, u, s):
                rows = aligned(base + j * 8)
                total = (squares + gx_ref[aligned(w_row(0, ib, j)), :]) + gz_ref[aligned(512 + base + j * 8), :]
                size = total * lax.rsqrt(jnp.maximum(total, 1e-35))
                moved = u + s * 3.0
                moved = jnp.where(s > 0.0, moved - size, moved + size)
                if stage == 1:
                    moved = 0.75 * wa[rows, :] + 0.25 * moved
                elif stage == 2:
                    moved = (1.0 / 3.0) * wa[rows, :] + (2.0 / 3.0) * moved
                if stage < 2:
                    n_ref[rows, :] = moved
                    ux_rows[x_rows(t, ib, j), :] = moved
                new[j] = moved
                if stage == 2 and j % 2 == 1:
                    a, b = new[j - 1], moved
                    m = j // 2
                    orow = aligned(ib * 8)
                    out_ref[t, orow, m * 128:(m + 1) * 128] = jnp.where(lanes_low, a, roll(b))
                    out_ref[t, orow, (m + 16) * 128:(m + 17) * 128] = jnp.where(lanes_low, roll(a), b)

            column(load, lambda j: s_ref[aligned(base + j * 8), :], emit, 32, between)

        def y_pair(t, q):
            it = t * 4 + q
            get_low = face_source(t, 2, yf)
            get_high = face_source(t, 3, yf)
            lows = [get_low(h, q) for h in range(3)]
            highs = [get_high(h, q) for h in range(3)]
            before = jnp.maximum(it - 1, 0)
            y_stream(t, q, 0, lows, highs, functools.partial(turn, before // 4, 2 * lax.rem(before, 4) + 1))
            y_stream(t, q, 1, lows, highs, functools.partial(turn, t, 2 * q))

        def turn(t, ib, j):
            if stage < 2 and j % 16 == 4:
                half = j // 16
                to_v([n_ref[aligned(w_row(t, ib, 16 * half + k)), :] for k in range(16)], t, ib, half)

        def tile(t, carry):
            lax.fori_loop(0, 2, x_pair, t)
            lax.fori_loop(0, 4, lambda q, kept: (y_pair(t, q), kept)[1], 0)
            return carry

        lax.fori_loop(0, SLOTS, tile, 0)
        for j in (4, 20):
            turn(3, 7, j)

    section(0, wa, wb, x_faces0, y_faces0)
    section(1, wb, wc, x_faces1, y_faces1)
    section(2, wc, None, x_faces2, y_faces2)


def finish(count_ref, moved_ref, out_ref, zero, sem):
    def each(act, filled):
        for t in range(SLOTS):
            @pl.when((t < count_ref[0]) == filled)
            def _():
                source = moved_ref.at[t] if filled else zero
                act(pltpu.make_async_copy(source, out_ref.at[t], sem.at[t]))

    each(lambda copy: copy.start(), True)
    zero[...] = jnp.zeros_like(zero)
    each(lambda copy: copy.start(), False)
    each(lambda copy: copy.wait(), True)
    each(lambda copy: copy.wait(), False)


def local(level_set, tile_count, neighbours):
    rows = lambda count: pltpu.VMEM((count, 128), jnp.float32)
    blocks = lambda count: pltpu.VMEM((count, 8, 128), jnp.float32)
    whole = SLOTS * EDGE ** 3 // 128
    scratch = [rows(whole), rows(whole), rows(whole), rows(whole), blocks(whole // 8), blocks(whole // 8),
               blocks(whole // 8), blocks(whole // 8),
               rows(whole // SLOTS), rows(whole + 512), rows(512), rows(512)]
    scratch += [blocks(4 * FACE) for _ in range(6)]
    scratch += [pltpu.SemaphoreType.DMA((3, 4)), pltpu.SemaphoreType.DMA((3, 4)), pltpu.SemaphoreType.DMA((SLOTS,))]
    cells = SLOTS * EDGE ** 3
    blocked = level_set.reshape(SLOTS, 8, 8, 32, 128).transpose(0, 1, 3, 2, 4).reshape(whole, 128)
    moved = pl.pallas_call(
        kernel,
        out_shape=jax.ShapeDtypeStruct(level_set.shape, jnp.float32),
        in_specs=[
            pl.BlockSpec(memory_space=pl.ANY),
            pl.BlockSpec(memory_space=pltpu.SMEM),
        ],
        out_specs=pl.BlockSpec(memory_space=pltpu.VMEM),
        scratch_shapes=scratch,
        compiler_params=pltpu.CompilerParams(
            collective_id=0, has_side_effects=True, vmem_limit_bytes=47 * 2 ** 20
        ),
        cost_estimate=pl.CostEstimate(flops=cells * 3 * 150, bytes_accessed=cells * 8, transcendentals=cells * 3),
    )(blocked, neighbours)
    return pl.pallas_call(
        finish,
        out_shape=jax.ShapeDtypeStruct(level_set.shape, jnp.float32),
        in_specs=[pl.BlockSpec(memory_space=pltpu.SMEM), pl.BlockSpec(memory_space=pl.ANY)],
        out_specs=pl.BlockSpec(memory_space=pl.ANY),
        scratch_shapes=[pltpu.VMEM(level_set.shape[1:], jnp.float32), pltpu.SemaphoreType.DMA((SLOTS,))],
        compiler_params=pltpu.CompilerParams(vmem_limit_bytes=8 * 2 ** 20),
    )(tile_count, moved)


def solution(mesh):
    placed = (P(("gx", "gy"), None, None), P(("gx", "gy")), P(("gx", "gy"), None))
    return jax.shard_map(
        local, mesh=mesh, in_specs=placed, out_specs=P(("gx", "gy"), None, None), check_vma=False
    )
```

```python
import functools

import jax
import jax.numpy as jnp
from jax import lax
from jax.experimental import pallas as pl
from jax.experimental.pallas import tpu as pltpu
from jax.sharding import PartitionSpec as P

weno_eps = 1e-06
pseudo_step = 0.3
scale_s = pseudo_step / 3.0

SLOTS = 4
EDGE = 64
FACE = SLOTS * 3 * 4


def rcp(x):
    return pl.reciprocal(x, approx=True)


def aligned(start, count=8):
    return pl.ds(pl.multiple_of(start, 8), count)


def column(load, load_s, emit, n, between=None):
    kept = {}

    def memo(name, p, make):
        key = (name, p)
        if key not in kept:
            kept[key] = make()
        return kept[key]

    U = lambda p: memo("u", p, lambda: load(p))
    D = lambda p: memo("d", p, lambda: U(p + 1) - U(p))
    E = lambda p: memo("e", p, lambda: D(p) - D(p - 1))
    EH = lambda p: memo("eh", p, lambda: E(p) * 0.5)
    FH = lambda p: memo("fh", p, lambda: EH(p + 1) - EH(p))
    GH = lambda p: memo("gh", p, lambda: FH(p) - FH(p - 1))
    G15 = lambda p: memo("g15", p, lambda: GH(p) * 1.5)
    FF = lambda p: memo("ff", p, lambda: (FH(p) * FH(p)) * (8.0 / 3.0) + 0.5 * weno_eps)
    SQ = lambda p: memo("sq", p, lambda: E(p) * E(p))
    PP = lambda p: memo("pp", p, lambda: E(p) * EH(p + 1))
    LOW = lambda p: memo("low", p, lambda: FF(p) - PP(p))

    def face(j):
        def make():
            ra = rcp(LOW(j - 2) + SQ(j - 1))
            rb = rcp(FF(j - 1) + PP(j - 1))
            c = LOW(j) + SQ(j)
            xr = c * ra
            yr = c * rb
            x = xr * xr
            y = (yr * yr) * 3.0
            w = x * 0.5 + y
            a = x * GH(j - 1)
            minus = (a + G15(j)) * rcp(w + 1.5)
            plus = (GH(j) + a * 1.5) * rcp((w + 0.5) + x)
            return minus, plus

        return memo("face", j, make)

    for i in range(n):
        qm = face(i)[0]
        qp = face(i + 1)[1]
        t = (U(i + 1) - U(i - 1)) + (D(i - 1) + EH(i - 1))
        s = load_s(i)
        w = jnp.maximum(jnp.maximum(s * (t - qm), s * ((GH(i) - t) - qp)), 0.0)
        emit(i, w * w, U(i), s)
        if between is not None:
            between(i)


def w_row(t, ib, j):
    return ((t * 8 + ib) * 32 + j) * 8


def v_block(t, block, k):
    return (t * 4 + block) * EDGE + k


def face_block(side, t, h, c):
    return ((side * SLOTS + t) * 3 + h) * 4 + c


def one_if_none(n):
    return jnp.maximum(-n, 0)


def one_if_far(n):
    return jnp.minimum(jnp.maximum(n - (SLOTS - 1), 0), 1)


def kernel(
    level_ref, nb_ref, out_ref,
    wa, wb, wc, s_ref, ux_ref, sx_ref, v_ref, sv_ref, gx_ref, gz_ref, gva, gvb,
    x_faces0, x_faces1, x_faces2, y_faces0, y_faces1, y_faces2, send_sem, recv_sem, load_sem,
):
    v_rows = v_ref.reshape(SLOTS * 4 * EDGE * 8, 128)
    ux_rows = ux_ref.reshape(SLOTS * 4 * EDGE * 8, 128)
    sx_rows = sx_ref.reshape(SLOTS * 4 * EDGE * 8, 128)
    sv_rows = sv_ref.reshape(SLOTS * 4 * EDGE * 8, 128)

    def x_rows(t, ib, j):
        return pl.ds(v_block(t, j // 8, ib * 8) * 8 + j % 8, 8, stride=8)
    gx, gy = lax.axis_index("gx"), lax.axis_index("gy")
    n_gx, n_gy = lax.axis_size("gx"), lax.axis_size("gy")
    x_low, x_high = lax.rem(gx + n_gx - 1, n_gx), lax.rem(gx + 1, n_gx)
    y_low, y_high = lax.rem(gy + n_gy - 1, n_gy), lax.rem(gy + 1, n_gy)
    lanes_low = lax.broadcasted_iota(jnp.int32, (8, 128), 1) < 64

    def roll(x):
        return pltpu.roll(x, 64, axis=1)

    tile_rows = [pl.ds(t * 2048, 2048) for t in range(SLOTS)]
    loads = [pltpu.make_async_copy(level_ref.at[r], wc.at[r], load_sem.at[t]) for t, r in enumerate(tile_rows)]
    for load in loads:
        load.start()

    barrier = pltpu.get_barrier_semaphore()
    around = ((x_low, gy), (x_high, gy), (gx, y_low), (gx, y_high))
    for device in around:
        pl.semaphore_signal(barrier, inc=1, device_id=device, device_id_type=pl.DeviceIdType.MESH)

    def to_v(values, t, ib, half, with_sign=False):
        turned = jnp.concatenate(values, axis=0).T
        for jh in range(2):
            line = lax.rem(ib, 2) * 4 + half * 2 + jh
            for m in range(8):
                r = jh * 64 + 8 * m
                start = v_block(t, ib // 2, 8 * m) * 8 + line
                u = turned[r:r + 8]
                v_rows[pl.ds(start, 8, stride=8), :] = u
                if with_sign:
                    sv_rows[pl.ds(start, 8, stride=8), :] = (u * scale_s) * lax.rsqrt(u * u + 1.0)

    def enter_block(t, ib):
        values = []
        for m in range(16):
            a = wc[aligned(w_row(t, ib, m)), :]
            b = wc[aligned(w_row(t, ib, m + 16)), :]
            values.append(jnp.where(lanes_low, a, roll(b)))
            values.append(jnp.where(lanes_low, roll(a), b))
        for j in range(32):
            u = values[j]
            wa[aligned(w_row(t, ib, j)), :] = u
            s = (u * scale_s) * lax.rsqrt(u * u + 1.0)
            s_ref[aligned(w_row(t, ib, j)), :] = s
            ux_rows[x_rows(t, ib, j), :] = u
            sx_rows[x_rows(t, ib, j), :] = s
        for half in range(2):
            to_v(values[16 * half:16 * half + 16], t, ib, half, True)

    for t in range(SLOTS):
        def enter(q, carry, t=t):
            for e in range(2):
                enter_block(t, 2 * q + e)
            return carry

        loads[t].wait()
        lax.fori_loop(0, 4, enter, 0)

    gvb[...] = jnp.zeros_like(gvb)
    pl.semaphore_wait(barrier, 4)

    def section(stage, u_ref, n_ref, xf, yf):
        def pack(t, carry):
            for side in range(2):
                for h in range(3):
                    i = h if side == 0 else 61 + h
                    for c in range(4):
                        xf[face_block(side, t, h, c)] = ux_ref[v_block(t, c, i)]
                    for q in range(4):
                        j = h if side == 0 else 29 + h
                        even = u_ref[aligned(w_row(t, 2 * q, j)), :]
                        odd = u_ref[aligned(w_row(t, 2 * q + 1, j)), :]
                        if side == 0:
                            both = jnp.where(lanes_low, even, roll(odd))
                        else:
                            both = jnp.where(lanes_low, roll(even), odd)
                        yf[face_block(side, t, h, q)] = both
            return carry

        lax.fori_loop(0, 4, pack, 0)
        low, high, below, above = (pl.ds(part * FACE, FACE) for part in range(4))
        plan = (
            (xf, high, below, (x_high, gy)), (xf, low, above, (x_low, gy)),
            (yf, high, below, (gx, y_high)), (yf, low, above, (gx, y_low)),
        )
        copies = []
        for f, (table, source, target, device) in enumerate(plan):
            copy = pltpu.make_async_remote_copy(
                src_ref=table.at[source], dst_ref=table.at[target], send_sem=send_sem.at[stage, f],
                recv_sem=recv_sem.at[stage, f], device_id=device, device_id_type=pl.DeviceIdType.MESH,
            )
            copy.start()
            copies.append(copy)

        def z_back(source, it, pair):
            parts = [source[pl.ds((8 * m + 2 * pair + jh) * 8, 8), :] for jh in range(2) for m in range(8)]
            gz_ref[aligned(512 + it * 512 + pair * 128, 128), :] = jnp.concatenate(parts, axis=0).T

        def z_stream(it, target, before):
            t, block = it // 4, lax.rem(it, 4)
            base = v_block(t, block, 0)

            def layer(n, own, other):
                none = one_if_none(n)
                return none * (t * 256 + own) + (1 - none) * (n * 256 + other) + block * EDGE

            n_low, n_high = nb_ref[t, 4], nb_ref[t, 5]

            def load(p):
                if p < 0:
                    return v_ref[layer(n_low, 0, 64 + p)]
                if p >= 64:
                    return v_ref[layer(n_high, 63, p - 64)]
                return v_ref[base + p]

            def emit(i, squares, u, s):
                target[pl.ds((i // 8) * 64 + i % 8, 8, stride=8), :] = squares

            def between(i):
                if i % 16 == 4:
                    z_back(before, it - 1, i // 16)

            column(load, lambda i: sv_ref[base + i], emit, 64, between)

        def z_pair(n, carry):
            z_stream(2 * n, gva, gvb)
            z_stream(2 * n + 1, gvb, gva)
            return carry

        lax.fori_loop(0, 8, z_pair, 0)
        for pair in range(4):
            z_back(gvb, 15, pair)

        for copy in copies:
            copy.wait()

        def face_source(t, f, table):
            n = nb_ref[t, f]
            own_side, other_side = (0, 1) if f % 2 == 0 else (1, 0)
            outer = 0 if f % 2 == 0 else 2
            none, far = one_if_none(n), one_if_far(n)
            own = none * face_block(own_side, t, outer, 0)
            near = (1 - none) * (1 - far) * face_block(other_side, n, 0, 0)
            away = far * ((2 + f % 2) * FACE + (n - SLOTS) * 12)

            def get(h, c):
                return table[own + near + away + (1 - none) * (4 * h) + c]

            return get

        def x_stream(t, c):
            get_low = face_source(t, 0, xf)
            get_high = face_source(t, 1, xf)

            base = v_block(t, c, 0)

            def load(p):
                if p < 0:
                    return get_low(p + 3, c)
                if p >= 64:
                    return get_high(p - 64, c)
                return ux_ref[base + p]

            def emit(i, squares, u, s):
                gx_ref[pl.ds(w_row(0, i // 8, 8 * c) + i % 8, 8, stride=8), :] = squares

            column(load, lambda i: sx_ref[base + i], emit, 64)

        def x_pair(n, t):
            x_stream(t, 2 * n)
            x_stream(t, 2 * n + 1)
            return t

        def y_stream(t, q, parity, lows, highs, between):
            ib = 2 * q + parity
            base = w_row(t, ib, 0)
            new = {}

            def load(p):
                if p < 0:
                    h = p + 3
                    halo = lows[h] if parity == 0 else roll(lows[h])
                    return jnp.where(lanes_low, halo, roll(u_ref[aligned(base + (29 + h) * 8), :]))
                if p >= 32:
                    h = p - 32
                    halo = roll(highs[h]) if parity == 0 else highs[h]
                    return jnp.where(lanes_low, roll(u_ref[aligned(base + h * 8), :]), halo)
                return u_ref[aligned(base + p * 8), :]

            def emit(j, squares, u, s):
                rows = aligned(base + j * 8)
                total = (squares + gx_ref[aligned(w_row(0, ib, j)), :]) + gz_ref[aligned(512 + base + j * 8), :]
                size = total * lax.rsqrt(jnp.maximum(total, 1e-35))
                moved = u + s * 3.0
                moved = jnp.where(s > 0.0, moved - size, moved + size)
                if stage == 1:
                    moved = 0.75 * wa[rows, :] + 0.25 * moved
                elif stage == 2:
                    moved = (1.0 / 3.0) * wa[rows, :] + (2.0 / 3.0) * moved
                if stage < 2:
                    n_ref[rows, :] = moved
                    ux_rows[x_rows(t, ib, j), :] = moved
                new[j] = moved
                if stage == 2 and j % 2 == 1:
                    a, b = new[j - 1], moved
                    m = j // 2
                    orow = aligned(ib * 8)
                    out_ref[t, orow, m * 128:(m + 1) * 128] = jnp.where(lanes_low, a, roll(b))
                    out_ref[t, orow, (m + 16) * 128:(m + 17) * 128] = jnp.where(lanes_low, roll(a), b)

            column(load, lambda j: s_ref[aligned(base + j * 8), :], emit, 32, between)

        def y_pair(t, q):
            it = t * 4 + q
            get_low = face_source(t, 2, yf)
            get_high = face_source(t, 3, yf)
            lows = [get_low(h, q) for h in range(3)]
            highs = [get_high(h, q) for h in range(3)]
            before = jnp.maximum(it - 1, 0)
            y_stream(t, q, 0, lows, highs, functools.partial(turn, before // 4, 2 * lax.rem(before, 4) + 1))
            y_stream(t, q, 1, lows, highs, functools.partial(turn, t, 2 * q))

        def turn(t, ib, j):
            if stage < 2 and j % 16 == 4:
                half = j // 16
                to_v([n_ref[aligned(w_row(t, ib, 16 * half + k)), :] for k in range(16)], t, ib, half)

        def tile(t, carry):
            lax.fori_loop(0, 2, x_pair, t)
            lax.fori_loop(0, 4, lambda q, kept: (y_pair(t, q), kept)[1], 0)
            return carry

        lax.fori_loop(0, SLOTS, tile, 0)
        for j in (4, 20):
            turn(3, 7, j)

    section(0, wa, wb, x_faces0, y_faces0)
    section(1, wb, wc, x_faces1, y_faces1)
    section(2, wc, None, x_faces2, y_faces2)


def finish(count_ref, moved_ref, out_ref, zero, sem):
    def each(act, filled):
        for t in range(SLOTS):
            @pl.when((t < count_ref[0]) == filled)
            def _():
                source = moved_ref.at[t] if filled else zero
                act(pltpu.make_async_copy(source, out_ref.at[t], sem.at[t]))

    each(lambda copy: copy.start(), True)
    zero[...] = jnp.zeros_like(zero)
    each(lambda copy: copy.start(), False)
    each(lambda copy: copy.wait(), True)
    each(lambda copy: copy.wait(), False)


def local(level_set, tile_count, neighbours):
    rows = lambda count: pltpu.VMEM((count, 128), jnp.float32)
    blocks = lambda count: pltpu.VMEM((count, 8, 128), jnp.float32)
    whole = SLOTS * EDGE ** 3 // 128
    scratch = [rows(whole), rows(whole), rows(whole), rows(whole), blocks(whole // 8), blocks(whole // 8),
               blocks(whole // 8), blocks(whole // 8),
               rows(whole // SLOTS), rows(whole + 512), rows(512), rows(512)]
    scratch += [blocks(4 * FACE) for _ in range(6)]
    scratch += [pltpu.SemaphoreType.DMA((3, 4)), pltpu.SemaphoreType.DMA((3, 4)), pltpu.SemaphoreType.DMA((SLOTS,))]
    cells = SLOTS * EDGE ** 3
    blocked = level_set.reshape(SLOTS, 8, 8, 32, 128).transpose(0, 1, 3, 2, 4).reshape(whole, 128)
    moved = pl.pallas_call(
        kernel,
        out_shape=jax.ShapeDtypeStruct(level_set.shape, jnp.float32),
        in_specs=[
            pl.BlockSpec(memory_space=pl.ANY),
            pl.BlockSpec(memory_space=pltpu.SMEM),
        ],
        out_specs=pl.BlockSpec(memory_space=pltpu.VMEM),
        scratch_shapes=scratch,
        compiler_params=pltpu.CompilerParams(
            collective_id=0, has_side_effects=True, vmem_limit_bytes=47 * 2 ** 20
        ),
        cost_estimate=pl.CostEstimate(flops=cells * 3 * 150, bytes_accessed=cells * 8, transcendentals=cells * 3),
    )(blocked, neighbours)
    return pl.pallas_call(
        finish,
        out_shape=jax.ShapeDtypeStruct(level_set.shape, jnp.float32),
        in_specs=[pl.BlockSpec(memory_space=pltpu.SMEM), pl.BlockSpec(memory_space=pl.ANY)],
        out_specs=pl.BlockSpec(memory_space=pl.ANY),
        scratch_shapes=[pltpu.VMEM(level_set.shape[1:], jnp.float32), pltpu.SemaphoreType.DMA((SLOTS,))],
        compiler_params=pltpu.CompilerParams(vmem_limit_bytes=8 * 2 ** 20),
    )(tile_count, moved)


def solution(mesh):
    placed = (P(("gx", "gy"), None, None), P(("gx", "gy")), P(("gx", "gy"), None))
    return jax.shard_map(
        local, mesh=mesh, in_specs=placed, out_specs=P(("gx", "gy"), None, None), check_vma=False
    )
```
